32 devices in a mesh: section: 4 (over y, x), group: 8 (over z, core).
Axes of the slice: x: 2, y: 2, z: 4, core: 2. Of those that a mesh axis runs over, the one named last changes fastest.
Arguments:
- hidden: bfloat16 [512, 8, 1024], P('group', None, 'section'), may hold values from -6 to 6
- pre_weight: bfloat16 [7, 1024, 512], replicated, may hold values from -0.0625 to 0.0625
- up1_weight: bfloat16 [16, 512, 256], replicated, may hold values from -0.1875 to 0.1875
- up2_weight: bfloat16 [16, 256, 128], replicated, may hold values from -0.25 to 0.25
- up3_weight: bfloat16 [4, 128, 64], replicated, may hold values from -0.375 to 0.375
- res3_weight: bfloat16 [3, 64, 64], replicated, may hold values from -0.4375 to 0.4375
- up4_weight: bfloat16 [4, 64, 32], replicated, may hold values from -0.5 to 0.5
- res4_weight: bfloat16 [3, 32, 32], replicated, may hold values from -0.625 to 0.625
- post_weight: bfloat16 [7, 32], replicated, may hold values from -0.375 to 0.375
- owner_device: int32 [512, 1], replicated, may hold values from 0 to 7; in each aligned block of 16 rows (0 to 15, 16 to 31, ...) at most 8 rows name the same one
- stream_slot: int32 [512], replicated, may hold values from 0 to 3
- start_frame: int32 [512], replicated, may hold values from 0 to 56
- lead_frames: int32 [512], replicated, may hold values from 1 to 4
- tail_frames: int32 [512], replicated, may hold values from 1 to 4
Outputs:
- waveform: float32 [32, 4, 16384], P('group', 'section')
The draws below stay inside these ranges and needn't reach their ends.
Inputs may be any that keep to these rules, and one draw needn't show every extreme that they name: `owner_device`: in each aligned block of 16 groups (the groups of one device), no owner is named by more than 8 groups, a bound that some block reaches.
All inputs are finite; a program needn't handle non-finite values.
Results may differ from the reference program's by a relative error of at most 0.015.
Values may be sent and summed in bfloat16 or wider, within the bound.
A program may use at most 128 MiB of HBM per device.

```python
import math
import jax
import jax.numpy as jnp
import numpy as np
from jax import lax

H = 1024
C0 = 512
C1 = 256
C2 = 128
C3 = 64
C4 = 32
FR = 8
OVF = 4
HOP = 256
CD = 16
STR_DEV = 4
SLF = 64
CAP = 8
GROUPS = 512
CL = 2048
SL = 16384
SROWS = 32
SECTIONS = 4
N_GROUP = 8


def plant(entries, key, least, high):
    longest = entries.shape.index(max(entries.shape))
    spots = []
    for shift in (0, 1):
        where = [jax.random.randint(jax.random.fold_in(key, axis), (), 0, length) for axis, length in enumerate(entries.shape)]
        where[longest] = (where[longest] + shift) % entries.shape[longest]
        spots.append(tuple(where))
    return entries.at[spots[0]].set(least).at[spots[1]].set(high)


def block_levels(key, dims, cuts, low, largest):
    loudness, own = 1.0, jax.random.fold_in(key, 6)
    for axis_at, shards_of in cuts:
        draws = jnp.exp(jax.random.uniform(jax.random.fold_in(own, axis_at), (shards_of,), jnp.float32, low / len(cuts), largest / len(cuts)))
        loudness = loudness * jnp.repeat(draws, dims[axis_at] // shards_of).reshape([-1 if axis == axis_at else 1 for axis in range(len(dims))])
    return loudness


def assign_block(own_key, own, number, rows, number_of, top, limit, skew):
    order = jax.random.permutation(own_key, number_of)
    crowded, usual = load_shares(number_of, rows * top, limit, skew, True), load_shares(number_of, rows * top, limit, skew, False)
    places = jnp.arange(number_of)

    def named(sizes, rotation):
        used = int((sizes > 0).sum())
        fixed = max(1, used // 4)
        passed = fixed + (places - fixed + rotation * (used - fixed)) % max(1, number_of - fixed)
        return jnp.zeros((number_of,), jnp.int32).at[order[jnp.where(places < fixed, places, passed)]].set(jnp.asarray(sizes, jnp.int32))

    sizes = jnp.where(number % 4 == 0, named(crowded, number // 4), named(usual, number - number // 4 - 1))
    mixed = jax.random.permutation(jax.random.fold_in(own, 3), number_of)
    giver, receiver = mixed[0:number_of // 2 * 2:2], mixed[1:number_of // 2 * 2:2]
    slack = jnp.minimum(sizes[giver] - 1, limit - sizes[receiver]) // 2
    slack = jnp.where((giver == order[0]) | (receiver == order[0]) | (sizes[receiver] == 0), 0, jnp.maximum(slack, 0))
    passed = jax.random.randint(jax.random.fold_in(own, 4), (number_of // 2,), 0, 1 << 20) % (slack + 1)
    sizes = sizes.at[giver].add(-passed).at[receiver].add(passed)
    members = jnp.searchsorted(jnp.cumsum(sizes), jnp.arange(rows * top), side="right").astype(jnp.int32)
    grid = members.reshape(top, rows).T
    grid = grid[jax.random.permutation(jax.random.fold_in(own, 1), rows)]
    rotation = jax.random.randint(jax.random.fold_in(own, 2), (rows, 1), 0, top)
    return jnp.take_along_axis(grid, (jnp.arange(top)[None, :] + rotation) % top, axis=1)


def load_shares(amount, total, bound, lean, full):
    portions = [(1 << 20) // math.isqrt(rank ** lean) + 1 for rank in range(1, amount + 1)]
    largest = bound if full else min(bound, max(-(-total // amount), total * portions[0] // sum(portions)))
    least = 1 if total - largest >= amount - 1 else 0
    given, surplus = [largest] + [least] * (amount - 1), total - largest - least * (amount - 1)
    while surplus > 0:
        candidates = [i for i in range(1, amount) if given[i] < largest] or [i for i in range(1, amount) if given[i] < bound]
        whole, budget = sum([portions[i] for i in candidates]), surplus
        for i in candidates:
            extra = min(bound - given[i], max(1, budget * portions[i] // whole), surplus)
            given[i] = given[i] + extra
            surplus = surplus - extra
    return np.array(given)


def gaussian(rng, dims, spread, reach, pieces=(), kind=jnp.bfloat16):
    result = spread * jax.random.normal(rng, dims, jnp.float32)
    if pieces:
        result = result * block_levels(rng, dims, pieces, -0.22, 0.18)
    return jnp.clip(result, -reach, reach).astype(kind)


def setup_inputs(seed: int = 0) -> dict:
    seeds = jax.random.split(jax.random.key(seed), 15)
    hidden = gaussian(seeds[0], (GROUPS, FR, H), 1.0, 6.0, ((0, 8), (2, 4)))
    pre_weight = gaussian(seeds[1], (7, H, C0), (7 * H) ** -0.5, 0.0625)
    up1_weight = gaussian(seeds[2], (16, C0, C1), (2 * C0) ** -0.5, 0.1875)
    up2_weight = gaussian(seeds[3], (16, C1, C2), (2 * C1) ** -0.5, 0.25)
    up3_weight = gaussian(seeds[4], (4, C2, C3), (2 * C2) ** -0.5, 0.375)
    res3_weight = gaussian(seeds[5], (3, C3, C3), (3 * C3) ** -0.5, 0.4375)
    up4_weight = gaussian(seeds[6], (4, C3, C4), (2 * C3) ** -0.5, 0.5)
    res4_weight = gaussian(seeds[7], (3, C4, C4), (3 * C4) ** -0.5, 0.625)
    post_weight = gaussian(seeds[8], (7, C4), (7 * C4) ** -0.5, 0.375)
    owner_device_keys = jax.random.split(jax.random.fold_in(seeds[9], 1), GROUPS // CD)
    owner_device_turns = jax.random.permutation(jax.random.fold_in(seeds[9], 3), GROUPS // CD)
    owner_device = jax.vmap(lambda own, number: assign_block(jax.random.fold_in(seeds[9], 2), own, number, CD, N_GROUP, 1, CAP, 2))(owner_device_keys, owner_device_turns).reshape((GROUPS, 1))
    stream_slot = plant(jax.random.randint(seeds[10], (GROUPS,), 0, STR_DEV), jax.random.fold_in(seeds[10], 1), 0, STR_DEV - 1).astype(jnp.int32)
    start_frame = plant(jax.random.randint(seeds[11], (GROUPS,), 0, SLF - FR + 1), jax.random.fold_in(seeds[11], 1), 0, SLF - FR).astype(jnp.int32)
    lead_frames = plant(jax.random.randint(seeds[12], (GROUPS,), 1, OVF + 1), jax.random.fold_in(seeds[12], 1), 1, OVF).astype(jnp.int32)
    tail_frames = plant(jax.random.randint(seeds[13], (GROUPS,), 1, OVF + 1), jax.random.fold_in(seeds[13], 1), 1, OVF).astype(jnp.int32)
    return {"hidden": hidden, "pre_weight": pre_weight, "up1_weight": up1_weight, "up2_weight": up2_weight, "up3_weight": up3_weight, "res3_weight": res3_weight, "up4_weight": up4_weight, "res4_weight": res4_weight, "post_weight": post_weight, "owner_device": owner_device, "stream_slot": stream_slot, "start_frame": start_frame, "lead_frames": lead_frames, "tail_frames": tail_frames}


exact_mode = lax.Precision.HIGHEST


def leaky_relu(values, slope):
    return jnp.where(values >= 0, values, slope * values)


def rounded(values):
    return lax.optimization_barrier(values.astype(jnp.bfloat16))


def as_float(values):
    return values.astype(jnp.float32)


def same_conv(inputs, weight, dilation):
    tap_count = weight.shape[0]
    pad_width = (tap_count - 1) // 2 * dilation
    length = inputs.shape[2]
    padded = jnp.pad(inputs, ((0, 0), (0, 0), (pad_width, pad_width)))
    summed = jnp.zeros((inputs.shape[0], weight.shape[2], length), jnp.float32)
    for tap_id in range(tap_count):
        shifted = padded[:, :, tap_id * dilation: tap_id * dilation + length]
        summed = summed + jnp.einsum("bcl,co->bol", shifted, weight[tap_id], precision=exact_mode)
    return summed


def transposed(inputs, weight, stride):
    batch_size = inputs.shape[0]
    length = inputs.shape[2]
    tap_count = weight.shape[0]
    widened = jnp.zeros((batch_size, weight.shape[2], (length - 1) * stride + tap_count), jnp.float32)
    for tap_id in range(tap_count):
        contrib = jnp.einsum("bcl,co->bol", inputs, weight[tap_id], precision=exact_mode)
        widened = widened.at[:, :, tap_id: tap_id + (length - 1) * stride + 1: stride].add(contrib)
    offset = stride // 2
    return widened[:, :, offset: offset + length * stride]


def window(lead, tail, length):
    sample = jnp.arange(length, dtype=jnp.float32) + 0.5
    ramp_in = jnp.minimum(1.0, sample[None, :] / (HOP * as_float(lead)[:, None]))
    ramp_out = jnp.minimum(1.0, (length - sample)[None, :] / (HOP * as_float(tail)[:, None]))
    return ramp_in * ramp_out


def vocode(rows_here, weights):
    pre_w, first_w, second_w, third_w, third_res, fourth_w, fourth_res, post_w = weights
    inputs = jnp.transpose(as_float(rows_here), (0, 2, 1))
    projected = same_conv(inputs, as_float(pre_w), 1)
    active = rounded(leaky_relu(projected, 0.1))
    upsampled = transposed(as_float(active), as_float(first_w), 8)
    active = rounded(leaky_relu(upsampled, 0.1))
    upsampled = transposed(as_float(active), as_float(second_w), 8)
    active = rounded(leaky_relu(upsampled, 0.1))
    upsampled = transposed(as_float(active), as_float(third_w), 2)
    inner_act = rounded(leaky_relu(upsampled, 0.1))
    middle = upsampled + same_conv(as_float(inner_act), as_float(third_res), 3)
    active = rounded(leaky_relu(middle, 0.1))
    upsampled = transposed(as_float(active), as_float(fourth_w), 2)
    inner_act = rounded(leaky_relu(upsampled, 0.1))
    middle = upsampled + same_conv(as_float(inner_act), as_float(fourth_res), 3)
    active = rounded(leaky_relu(middle, 0.01))
    output_conv = same_conv(as_float(active), as_float(post_w)[:, :, None], 1)[:, 0]
    return jnp.tanh(output_conv)


def reference(hidden, pre_weight, up1_weight, up2_weight, up3_weight, res3_weight, up4_weight, res4_weight, post_weight, owner_device, stream_slot, start_frame, lead_frames, tail_frames):
    weights = (pre_weight, up1_weight, up2_weight, up3_weight, res3_weight, up4_weight, res4_weight, post_weight)
    blocks = GROUPS // CD

    def vocode_block(operands):
        rows_here, lead_here, tail_here = operands
        return vocode(rows_here, weights) * window(lead_here, tail_here, CL)

    waves = lax.map(vocode_block, (hidden.reshape(blocks, CD, FR, H), lead_frames.reshape(blocks, CD), tail_frames.reshape(blocks, CD)))
    waves = waves.reshape(GROUPS, CL)
    row_index = (owner_device[:, 0] * STR_DEV + stream_slot).astype(jnp.int32)
    sections = ((jnp.arange(GROUPS, dtype=jnp.int32) // CD) % SECTIONS).astype(jnp.int32)
    offsets = (start_frame * HOP).astype(jnp.int32)

    def add_group(group_id, streams):
        corner = (row_index[group_id], sections[group_id], offsets[group_id])
        current = lax.dynamic_slice(streams, corner, (1, 1, CL))
        return lax.dynamic_update_slice(streams, current + waves[group_id].reshape(1, 1, CL), corner)

    return lax.fori_loop(0, GROUPS, add_group, jnp.zeros((SROWS, SECTIONS, SL), jnp.float32))
```

```python
import functools

import jax
import jax.numpy as jnp
from jax import lax
from jax.experimental import pallas as pl
from jax.experimental.pallas import tpu as pltpu
from jax.sharding import PartitionSpec as P

HOP = 256
STR_DEV = 4
SLF = 64
PAIRS = 32
CHUNK = 4
MESH = pl.DeviceIdType.MESH
F32 = jnp.float32
BF16 = jnp.bfloat16


def leaky(values, slope):
    return jnp.maximum(values, slope * values)


def iota(shape, dim):
    return lax.broadcasted_iota(jnp.int32, shape, dim)


def dot(lhs, rhs):
    return jnp.dot(lhs, rhs, preferred_element_type=F32)


def dot_nt(lhs, rhs):
    return lax.dot_general(lhs, rhs, (((1,), (1,)), ((), ())), preferred_element_type=F32)


def shifted(values, step, frames):
    rows = values.shape[0]
    frame = iota(values.shape, 0) & (frames - 1)
    moved = pltpu.roll(values, (-step) % rows, 0)
    inside = (frame + step >= 0) & (frame + step < frames)
    return jnp.where(inside, moved, 0.0)


def assemble(out_ref, spread, times, columns, tap_of):
    depth, width = spread[0].shape
    per_column = width // len(columns)
    column = iota((depth, width), 1) // per_column
    for place, time in enumerate(times):
        block = jnp.zeros((depth, width), F32)
        for at, out_time in enumerate(columns):
            tap = tap_of(time, out_time)
            if tap is not None:
                block = jnp.where(column == at, spread[tap], block)
        out_ref[place * depth : (place + 1) * depth, :] = block.astype(BF16)


def spread_taps(w_ref, copies):
    taps, _, width = w_ref.shape
    lanes = width * copies
    repeat = ((iota((width, lanes), 1) & (width - 1)) == iota((width, lanes), 0)).astype(F32).astype(BF16)
    return [dot(w_ref[tap], repeat) for tap in range(taps)]


def up_tap(time, out_time):
    tap = out_time + 1 - 2 * time
    return tap if 0 <= tap < 4 else None


def res_tap(time, out_time):
    step = time - out_time
    return step // 3 + 1 if step in (-3, 0, 3) else None


def kernel(
    sections,
    lanes,
    hidden_ref,
    pre_hbm,
    up1_hbm,
    up2_hbm,
    up3_ref,
    res3_ref,
    up4_ref,
    res4_ref,
    post_ref,
    owner_ref,
    slot_ref,
    start_ref,
    lead_ref,
    tail_ref,
    out_ref,
    x_ref,
    pre_ref,
    up1_ref,
    up2_ref,
    a1_ref,
    a_ref,
    i_ref,
    u_ref,
    w3_ref,
    r3_ref,
    w4_ref,
    r4_ref,
    wp_ref,
    place_ref,
    wave_ref,
    weight_sem,
    own_sem,
    hid_send,
    hid_recv,
    wave_send,
    wave_recv,
    fwd_send,
    fwd_recv,
):
    section = lax.axis_index("section")
    lane = lax.axis_index("group")
    chips = lanes // 2
    chip, core = lane // 2, lane % 2
    sibling = chip * 2 + (1 - core)
    rows = x_ref.shape[0] // sections
    frames = 8
    groups = rows // frames

    def block(index):
        return pl.ds(pl.multiple_of(index * rows, rows), rows)

    copies = [
        pltpu.make_async_copy(pre_hbm, pre_ref, weight_sem.at[0]),
        pltpu.make_async_copy(up1_hbm, up1_ref, weight_sem.at[1]),
        pltpu.make_async_copy(up2_hbm, up2_ref, weight_sem.at[2]),
    ]
    own = pltpu.make_async_copy(hidden_ref.at[block(section)], x_ref.at[block(section)], own_sem)

    barrier = pltpu.get_barrier_semaphore()
    for step in range(1, sections):
        pl.semaphore_signal(
            barrier, inc=1, device_id={"section": (section + step) % sections}, device_id_type=MESH
        )
    for step in range(1, chips):
        pl.semaphore_signal(
            barrier, inc=1, device_id={"group": ((chip + step) % chips) * 2 + core}, device_id_type=MESH
        )
    pl.semaphore_signal(barrier, inc=1, device_id={"group": sibling}, device_id_type=MESH)
    own.start()
    for copy in copies:
        copy.start()
    pl.semaphore_wait(barrier, sections + chips - 1)

    hidden_copies = []
    for step in range(1, sections):
        peer = (section + step) % sections
        hidden_copies.append(
            pltpu.make_async_remote_copy(
                src_ref=hidden_ref.at[block(peer)],
                dst_ref=x_ref.at[block(section)],
                send_sem=hid_send.at[step],
                recv_sem=hid_recv.at[step],
                device_id={"section": peer},
                device_id_type=MESH,
            )
        )
        hidden_copies[-1].start()

    assemble(w3_ref, spread_taps(up3_ref, 4), range(-1, 3), range(4), up_tap)
    assemble(r3_ref, spread_taps(res3_ref, 4), range(-4, 8), range(4), res_tap)
    assemble(w4_ref, spread_taps(up4_ref, 8), range(-2, 6), range(8), up_tap)
    assemble(r4_ref, spread_taps(res4_ref, 8), range(-4, 12), range(8), res_tap)
    post = post_ref[...].astype(F32)
    channels = post.shape[1]
    span = CHUNK * HOP // PAIRS
    eye = (iota((channels, channels), 0) == iota((channels, channels), 1)).astype(F32).astype(BF16)
    post_taps = [
        dot_nt(eye, jnp.broadcast_to(post[tap : tap + 1], (128, channels)).astype(BF16)) for tap in range(7)
    ]
    out_time = iota((channels, 128), 1) & (span - 1)
    for place, time in enumerate(range(-4, span + 4)):
        entry = jnp.zeros((channels, 128), F32)
        for tap in range(7):
            entry = jnp.where(out_time == time - tap + 3, post_taps[tap], entry)
        wp_ref[place * channels : (place + 1) * channels, :] = entry.astype(BF16)

    total = owner_ref.shape[1]
    which = iota((16, total), 0)
    facts = jnp.where(
        which == 0,
        owner_ref[...],
        jnp.where(
            which == 1,
            slot_ref[...] * SLF + start_ref[...],
            jnp.where(which == 2, lead_ref[...], jnp.where(which == 3, tail_ref[...], 0)),
        ),
    )
    facts = facts.astype(F32).astype(BF16)
    lane_groups = sections * groups
    per_tile = 128 // lane_groups
    row_group = iota((rows, total), 0) // frames
    mine = (iota((rows, total), 1) == lane * lane_groups + section * groups + row_group).astype(F32).astype(BF16)
    fades = dot_nt(mine, facts)
    lead, tail = fades[:, 2:3], fades[:, 3:4]
    column_group = iota((128, rows), 1) // frames
    column_frame = iota((1, rows), 1) & (frames - 1)
    target_row = iota((STR_DEV * SLF, rows), 0)
    for sub in range(per_tile):
        pick = (iota((128, rows), 0) == sub * lane_groups + section * groups + column_group).astype(F32).astype(BF16)
        for tile in range(total // 128):
            source = tile * per_tile + sub
            found = dot(facts[:, tile * 128 : (tile + 1) * 128], pick)
            owner = found[0:1].astype(jnp.int32)
            target = jnp.where(owner == lane, found[1:2].astype(jnp.int32) + column_frame, -1)
            place_ref[:, source * rows : (source + 1) * rows] = (
                (target_row == target).astype(F32).astype(BF16)
            )

    own.wait()
    copies[0].wait()
    for copy in hidden_copies:
        copy.wait()
    x = jnp.concatenate([x_ref[part * rows : (part + 1) * rows, :] for part in range(sections)], axis=1)
    projected = dot(x, pre_ref[3])
    for tap in (0, 1, 2, 4, 5, 6):
        projected = projected + shifted(dot(x, pre_ref[tap]), tap - 3, frames)
    active = leaky(projected, 0.1)
    now = active.astype(BF16)
    before = shifted(active, -1, frames).astype(BF16)
    after = shifted(active, 1, frames).astype(BF16)

    copies[1].wait()
    for phase in range(8):
        other, tap = (before, phase + 12) if phase < 4 else (after, phase - 4)
        up = dot(now, up1_ref[phase + 4]) + dot(other, up1_ref[tap])
        a1_ref[(phase + 1) * rows : (phase + 2) * rows, :] = leaky(up, 0.1).astype(BF16)

    def fill_ends(ref, count):
        last = ref[count * rows : (count + 1) * rows, :].astype(F32)
        ref[0:rows, :] = shifted(last, -1, frames).astype(BF16)
        first = ref[rows : 2 * rows, :].astype(F32)
        ref[(count + 1) * rows : (count + 2) * rows, :] = shifted(first, 1, frames).astype(BF16)

    fill_ends(a1_ref, 8)

    copies[2].wait()
    for pair in range(4):
        near = 2 * pair + 4
        far, offset = (2 * pair + 12, 0) if pair < 2 else (2 * pair - 4, 2)
        near_w = jnp.concatenate([up2_ref[near], up2_ref[near + 1]], axis=1)
        far_w = jnp.concatenate([up2_ref[far], up2_ref[far + 1]], axis=1)
        for half in range(2):
            low = half * 4
            here = a1_ref[(low + 1) * rows : (low + 5) * rows, :]
            there = a1_ref[(low + offset) * rows : (low + offset + 4) * rows, :]
            up = leaky(dot(here, near_w) + dot(there, far_w), 0.1).astype(BF16)
            for phase in range(4):
                to = (low + phase) * 4 + pair + 1
                a_ref[to * rows : (to + 1) * rows, :] = up[phase * rows : (phase + 1) * rows]
    fill_ends(a_ref, PAIRS)

    size = CHUNK * rows

    def each_chunk(body):
        def step(chunk, carry):
            body(pl.multiple_of(chunk * size, size))
            return carry

        lax.fori_loop(0, PAIRS // CHUNK, step, 0)

    def around(ref, at, whole):
        low = ref[pl.ds(at, size), :]
        mid = ref[pl.ds(pl.multiple_of(at + rows, rows), size), :]
        high = ref[pl.ds(pl.multiple_of(at + 2 * rows, rows), size), :]
        if not whole:
            low, high = low[:, 128:], high[:, :128]
        return jnp.concatenate([low, mid, high], axis=1)

    def upsample(w_ref):
        def body(at):
            up = dot(around(a_ref, at, False), w_ref[...])
            u_ref[pl.ds(at, size), :] = up
            i_ref[pl.ds(pl.multiple_of(at + rows, rows), size), :] = leaky(up, 0.1).astype(BF16)

        each_chunk(body)
        fill_ends(i_ref, PAIRS)

    def residual(w_ref, whole, slope):
        def body(at):
            middle = u_ref[pl.ds(at, size), :] + dot(around(i_ref, at, whole), w_ref[...])
            a_ref[pl.ds(pl.multiple_of(at + rows, rows), size), :] = leaky(middle, slope).astype(BF16)

        each_chunk(body)
        fill_ends(a_ref, PAIRS)

    upsample(w3_ref)
    residual(r3_ref, True, 0.1)
    upsample(w4_ref)
    residual(r4_ref, False, 0.01)

    post_w = wp_ref[...]
    halves = []
    column = iota((rows, 128), 1) // span
    for half in range(2):
        merged = jnp.zeros((rows, 128), F32)
        for part in range(128 // span):
            first = (half * (128 // span) + part) * CHUNK
            pieces = [a_ref[first * rows : (first + 1) * rows, 128:]]
            pieces += [a_ref[(first + 1 + p) * rows : (first + 2 + p) * rows, :] for p in range(CHUNK)]
            pieces += [a_ref[(first + 1 + CHUNK) * rows : (first + 2 + CHUNK) * rows, :128]]
            merged = jnp.where(column == part, dot(jnp.concatenate(pieces, axis=1), post_w), merged)
        halves.append(merged)
    wave = jnp.tanh(jnp.concatenate(halves, axis=1))
    frame = iota((rows, HOP), 0) & (frames - 1)
    sample = (frame * HOP + iota((rows, HOP), 1)).astype(F32) + 0.5
    ramp_in = jnp.minimum(1.0, sample / (HOP * lead))
    ramp_out = jnp.minimum(1.0, (frames * HOP - sample) / (HOP * tail))
    wave_ref[block(lane), :] = (wave * (ramp_in * ramp_out)).astype(BF16)

    def send(index, peer, send_sem, recv_sem):
        return pltpu.make_async_remote_copy(
            src_ref=wave_ref.at[block(index)],
            dst_ref=wave_ref.at[block(index)],
            send_sem=send_sem,
            recv_sem=recv_sem,
            device_id={"group": peer},
            device_id_type=MESH,
        )

    direct = []
    for step in range(1, chips):
        direct.append(send(lane, ((chip + step) % chips) * 2 + core, wave_send.at[step], wave_recv.at[step]))
        direct[-1].start()
    to_sibling = [send(lane, sibling, fwd_send.at[0], fwd_recv.at[0])]
    to_sibling[0].start()
    for step in range(1, chips):
        direct[step - 1].wait_recv()
        source = ((chip - step + chips) % chips) * 2 + core
        to_sibling.append(send(source, sibling, fwd_send.at[step], fwd_recv.at[step]))
        to_sibling[-1].start()
    for copy in to_sibling:
        copy.wait_recv()
    placed = dot(place_ref[...], wave_ref[...])
    out_ref[pl.ds(0, STR_DEV * SLF, stride=2), :] = placed[:, :128]
    out_ref[pl.ds(1, STR_DEV * SLF, stride=2), :] = placed[:, 128:]
    for copy in direct + to_sibling:
        copy.wait_send()


def shards(
    hidden,
    pre_weight,
    up1_weight,
    up2_weight,
    up3_weight,
    res3_weight,
    up4_weight,
    res4_weight,
    post_weight,
    owner_device,
    stream_slot,
    start_frame,
    lead_frames,
    tail_frames,
):
    sections = lax.axis_size("section")
    lanes = lax.axis_size("group")
    per_device = hidden.shape[0] // sections
    frames, width = hidden.shape[1], hidden.shape[2]
    rows = per_device * frames
    chips = lanes // 2
    total = stream_slot.shape[0]
    vmem = pl.BlockSpec(memory_space=pltpu.VMEM)
    hbm = pl.BlockSpec(memory_space=pl.ANY)
    blocks = PAIRS + 2
    out = pl.pallas_call(
        functools.partial(kernel, sections, lanes),
        out_shape=jax.ShapeDtypeStruct((STR_DEV * SLF * HOP // 128, 128), F32),
        in_specs=[hbm] * 4 + [vmem] * 10,
        out_specs=vmem,
        scratch_shapes=[
            pltpu.VMEM((sections * rows, width), BF16),
            pltpu.VMEM(pre_weight.shape, BF16),
            pltpu.VMEM(up1_weight.shape, BF16),
            pltpu.VMEM(up2_weight.shape, BF16),
            pltpu.VMEM((10 * rows, 256), BF16),
            pltpu.VMEM((blocks * rows, 256), BF16),
            pltpu.VMEM((blocks * rows, 256), BF16),
            pltpu.VMEM((PAIRS * rows, 256), F32),
            pltpu.VMEM((512, 256), BF16),
            pltpu.VMEM((768, 256), BF16),
            pltpu.VMEM((512, 256), BF16),
            pltpu.VMEM((512, 256), BF16),
            pltpu.VMEM(((CHUNK * HOP // PAIRS + 8) * 32, 128), BF16),
            pltpu.VMEM((STR_DEV * SLF, lanes * rows), BF16),
            pltpu.VMEM((lanes * rows, HOP), BF16),
            pltpu.SemaphoreType.DMA((3,)),
            pltpu.SemaphoreType.DMA,
            pltpu.SemaphoreType.DMA((sections,)),
            pltpu.SemaphoreType.DMA((sections,)),
            pltpu.SemaphoreType.DMA((chips,)),
            pltpu.SemaphoreType.DMA((chips,)),
            pltpu.SemaphoreType.DMA((chips,)),
            pltpu.SemaphoreType.DMA((chips,)),
        ],
        compiler_params=pltpu.CompilerParams(
            collective_id=0, has_side_effects=True, vmem_limit_bytes=48 * 1024 * 1024
        ),
        name="vocoder",
    )(
        hidden.reshape(sections * rows, width),
        pre_weight,
        up1_weight,
        up2_weight,
        up3_weight,
        res3_weight,
        up4_weight,
        res4_weight,
        post_weight,
        owner_device.reshape(1, total),
        stream_slot.reshape(1, total),
        start_frame.reshape(1, total),
        lead_frames.reshape(1, total),
        tail_frames.reshape(1, total),
    )
    return out.reshape(STR_DEV, 1, SLF * HOP)


def solution(mesh):
    in_specs = (P("group", None, "section"),) + (P(),) * 13
    return jax.shard_map(
        shards, mesh=mesh, in_specs=in_specs, out_specs=P("group", "section", None), check_vma=False
    )
```

```python
import functools

import jax
import jax.numpy as jnp
from jax import lax
from jax.experimental import pallas as pl
from jax.experimental.pallas import tpu as pltpu
from jax.sharding import PartitionSpec as P

HOP = 256
STR_DEV = 4
SLF = 64
PAIRS = 32
CHUNK = 4
MESH = pl.DeviceIdType.MESH
F32 = jnp.float32
BF16 = jnp.bfloat16


def leaky(values, slope):
    return jnp.maximum(values, slope * values)


def iota(shape, dim):
    return lax.broadcasted_iota(jnp.int32, shape, dim)


def dot(lhs, rhs):
    return jnp.dot(lhs, rhs, preferred_element_type=F32)


def dot_nt(lhs, rhs):
    return lax.dot_general(lhs, rhs, (((1,), (1,)), ((), ())), preferred_element_type=F32)


def dot_tn(lhs, rhs):
    return lax.dot_general(lhs, rhs, (((0,), (0,)), ((), ())), preferred_element_type=F32)


def shifted(values, step, frames):
    rows = values.shape[0]
    frame = iota(values.shape, 0) & (frames - 1)
    moved = pltpu.roll(values, (-step) % rows, 0)
    inside = (frame + step >= 0) & (frame + step < frames)
    return jnp.where(inside, moved, 0.0)


def assemble(out_ref, spread, times, columns, tap_of):
    depth, width = spread[0].shape
    per_column = width // len(columns)
    column = iota((depth, width), 1) // per_column
    for place, time in enumerate(times):
        block = jnp.zeros((depth, width), F32)
        for at, out_time in enumerate(columns):
            tap = tap_of(time, out_time)
            if tap is not None:
                block = jnp.where(column == at, spread[tap], block)
        out_ref[place * depth : (place + 1) * depth, :] = block.astype(BF16)


def spread_taps(w_ref, copies, flipped):
    taps, width = w_ref.shape[0], w_ref.shape[1 if flipped else 2]
    lanes = width * copies
    repeat = ((iota((width, lanes), 1) & (width - 1)) == iota((width, lanes), 0)).astype(F32).astype(BF16)
    return [(dot_tn if flipped else dot)(w_ref[tap], repeat) for tap in range(taps)]


def up_tap(time, out_time):
    tap = out_time + 1 - 2 * time
    return tap if 0 <= tap < 4 else None


def res_tap(time, out_time):
    step = time - out_time
    return step // 3 + 1 if step in (-3, 0, 3) else None


def kernel(
    sections,
    lanes,
    hidden_ref,
    pre_hbm,
    up1_hbm,
    up2_hbm,
    up3_ref,
    res3_ref,
    up4_ref,
    res4_ref,
    post_ref,
    owner_ref,
    slot_ref,
    start_ref,
    lead_ref,
    tail_ref,
    out_ref,
    x_ref,
    pre_ref,
    up1_ref,
    up2_ref,
    a1_ref,
    a_ref,
    i_ref,
    u_ref,
    w3_ref,
    r3_ref,
    w4_ref,
    r4_ref,
    wp_ref,
    place_ref,
    wave_ref,
    weight_sem,
    own_sem,
    hid_send,
    hid_recv,
    wave_send,
    wave_recv,
    fwd_send,
    fwd_recv,
):
    section = lax.axis_index("section")
    lane = lax.axis_index("group")
    chips = lanes // 2
    chip, core = lane // 2, lane % 2
    sibling = chip * 2 + (1 - core)
    rows = x_ref.shape[0] // sections
    frames = 8
    groups = rows // frames

    def block(index):
        return pl.ds(pl.multiple_of(index * rows, rows), rows)

    copies = [
        pltpu.make_async_copy(pre_hbm, pre_ref, weight_sem.at[0]),
        pltpu.make_async_copy(up1_hbm, up1_ref, weight_sem.at[1]),
        pltpu.make_async_copy(up2_hbm, up2_ref, weight_sem.at[2]),
    ]
    own = pltpu.make_async_copy(hidden_ref.at[block(section)], x_ref.at[block(section)], own_sem)

    barrier = pltpu.get_barrier_semaphore()
    for step in range(1, sections):
        pl.semaphore_signal(
            barrier, inc=1, device_id={"section": (section + step) % sections}, device_id_type=MESH
        )
    for step in range(1, chips):
        pl.semaphore_signal(
            barrier, inc=1, device_id={"group": ((chip + step) % chips) * 2 + core}, device_id_type=MESH
        )
    pl.semaphore_signal(barrier, inc=1, device_id={"group": sibling}, device_id_type=MESH)
    own.start()
    for copy in copies:
        copy.start()
    pl.semaphore_wait(barrier, sections + chips - 1)

    hidden_copies = []
    for step in range(1, sections):
        peer = (section + step) % sections
        hidden_copies.append(
            pltpu.make_async_remote_copy(
                src_ref=hidden_ref.at[block(peer)],
                dst_ref=x_ref.at[block(section)],
                send_sem=hid_send.at[step],
                recv_sem=hid_recv.at[step],
                device_id={"section": peer},
                device_id_type=MESH,
            )
        )
        hidden_copies[-1].start()

    assemble(w3_ref, spread_taps(up3_ref, 4, True), range(-1, 3), range(4), up_tap)
    assemble(r3_ref, spread_taps(res3_ref, 4, False), range(-4, 8), range(4), res_tap)
    assemble(w4_ref, spread_taps(up4_ref, 8, True), range(-2, 6), range(8), up_tap)
    assemble(r4_ref, spread_taps(res4_ref, 8, False), range(-4, 12), range(8), res_tap)
    post = post_ref[...].astype(F32)
    channels = post.shape[1]
    span = CHUNK * HOP // PAIRS
    eye = (iota((channels, channels), 0) == iota((channels, channels), 1)).astype(F32).astype(BF16)
    post_taps = [
        dot_nt(eye, jnp.broadcast_to(post[tap : tap + 1], (128, channels)).astype(BF16)) for tap in range(7)
    ]
    out_time = iota((channels, 128), 1) & (span - 1)
    for place, time in enumerate(range(-4, span + 4)):
        entry = jnp.zeros((channels, 128), F32)
        for tap in range(7):
            entry = jnp.where(out_time == time - tap + 3, post_taps[tap], entry)
        wp_ref[place * channels : (place + 1) * channels, :] = entry.astype(BF16)

    total = owner_ref.shape[1]
    which = iota((16, total), 0)
    facts = jnp.where(
        which == 0,
        owner_ref[...],
        jnp.where(
            which == 1,
            slot_ref[...] * SLF + start_ref[...],
            jnp.where(which == 2, lead_ref[...], jnp.where(which == 3, tail_ref[...], 0)),
        ),
    )
    facts = facts.astype(F32).astype(BF16)
    lane_groups = sections * groups
    per_tile = 128 // lane_groups
    row_group = iota((rows, total), 0) // frames
    mine = (iota((rows, total), 1) == lane * lane_groups + section * groups + row_group).astype(F32).astype(BF16)
    fades = dot_nt(mine, facts)
    lead, tail = fades[:, 2:3], fades[:, 3:4]
    column_group = iota((128, rows), 1) // frames
    column_frame = iota((1, rows), 1) & (frames - 1)
    target_row = iota((STR_DEV * SLF, rows), 0)
    for sub in range(per_tile):
        pick = (iota((128, rows), 0) == sub * lane_groups + section * groups + column_group).astype(F32).astype(BF16)
        for tile in range(total // 128):
            source = tile * per_tile + sub
            found = dot(facts[:, tile * 128 : (tile + 1) * 128], pick)
            owner = found[0:1].astype(jnp.int32)
            target = jnp.where(owner == lane, found[1:2].astype(jnp.int32) + column_frame, -1)
            place_ref[:, source * rows : (source + 1) * rows] = (
                (target_row == target).astype(F32).astype(BF16)
            )

    own.wait()
    copies[0].wait()
    for copy in hidden_copies:
        copy.wait()
    x = jnp.concatenate([x_ref[part * rows : (part + 1) * rows, :] for part in range(sections)], axis=1)
    projected = dot(x, pre_ref[3])
    for tap in (0, 1, 2, 4, 5, 6):
        projected = projected + shifted(dot(x, pre_ref[tap]), tap - 3, frames)
    active = leaky(projected, 0.1)
    now = active.astype(BF16)
    before = shifted(active, -1, frames).astype(BF16)
    after = shifted(active, 1, frames).astype(BF16)

    copies[1].wait()
    for phase in range(8):
        other, tap = (before, phase + 12) if phase < 4 else (after, phase - 4)
        up = dot(now, up1_ref[phase + 4]) + dot(other, up1_ref[tap])
        a1_ref[(phase + 1) * rows : (phase + 2) * rows, :] = leaky(up, 0.1).astype(BF16)

    def fill_ends(ref, count):
        last = ref[count * rows : (count + 1) * rows, :].astype(F32)
        ref[0:rows, :] = shifted(last, -1, frames).astype(BF16)
        first = ref[rows : 2 * rows, :].astype(F32)
        ref[(count + 1) * rows : (count + 2) * rows, :] = shifted(first, 1, frames).astype(BF16)

    fill_ends(a1_ref, 8)

    copies[2].wait()
    for pair in range(4):
        near = 2 * pair + 4
        far, offset = (2 * pair + 12, 0) if pair < 2 else (2 * pair - 4, 2)
        near_w = jnp.concatenate([up2_ref[near], up2_ref[near + 1]], axis=1)
        far_w = jnp.concatenate([up2_ref[far], up2_ref[far + 1]], axis=1)
        for half in range(2):
            low = half * 4
            here = a1_ref[(low + 1) * rows : (low + 5) * rows, :]
            there = a1_ref[(low + offset) * rows : (low + offset + 4) * rows, :]
            up = leaky(dot(here, near_w) + dot(there, far_w), 0.1).astype(BF16)
            for phase in range(4):
                to = (low + phase) * 4 + pair + 1
                a_ref[to * rows : (to + 1) * rows, :] = up[phase * rows : (phase + 1) * rows]
    fill_ends(a_ref, PAIRS)

    size = CHUNK * rows

    def each_chunk(body):
        def step(chunk, carry):
            body(pl.multiple_of(chunk * size, size))
            return carry

        lax.fori_loop(0, PAIRS // CHUNK, step, 0, unroll=True)

    def around(ref, at, whole):
        low = ref[pl.ds(at, size), :]
        mid = ref[pl.ds(pl.multiple_of(at + rows, rows), size), :]
        high = ref[pl.ds(pl.multiple_of(at + 2 * rows, rows), size), :]
        if not whole:
            low, high = low[:, 128:], high[:, :128]
        return jnp.concatenate([low, mid, high], axis=1)

    def upsample(w_ref):
        def body(at):
            up = dot(around(a_ref, at, False), w_ref[...])
            u_ref[pl.ds(at, size), :] = up
            i_ref[pl.ds(pl.multiple_of(at + rows, rows), size), :] = leaky(up, 0.1).astype(BF16)

        each_chunk(body)
        fill_ends(i_ref, PAIRS)

    def residual(w_ref, whole, slope):
        def body(at):
            middle = u_ref[pl.ds(at, size), :] + dot(around(i_ref, at, whole), w_ref[...])
            a_ref[pl.ds(pl.multiple_of(at + rows, rows), size), :] = leaky(middle, slope).astype(BF16)

        each_chunk(body)
        fill_ends(a_ref, PAIRS)

    upsample(w3_ref)
    residual(r3_ref, True, 0.1)
    upsample(w4_ref)
    residual(r4_ref, False, 0.01)

    post_w = wp_ref[...]
    halves = []
    column = iota((rows, 128), 1) // span
    for half in range(2):
        merged = jnp.zeros((rows, 128), F32)
        for part in range(128 // span):
            first = (half * (128 // span) + part) * CHUNK
            pieces = [a_ref[first * rows : (first + 1) * rows, 128:]]
            pieces += [a_ref[(first + 1 + p) * rows : (first + 2 + p) * rows, :] for p in range(CHUNK)]
            pieces += [a_ref[(first + 1 + CHUNK) * rows : (first + 2 + CHUNK) * rows, :128]]
            merged = jnp.where(column == part, dot(jnp.concatenate(pieces, axis=1), post_w), merged)
        halves.append(merged)
    wave = jnp.tanh(jnp.concatenate(halves, axis=1))
    frame = iota((rows, HOP), 0) & (frames - 1)
    sample = (frame * HOP + iota((rows, HOP), 1)).astype(F32) + 0.5
    ramp_in = jnp.minimum(1.0, sample / (HOP * lead))
    ramp_out = jnp.minimum(1.0, (frames * HOP - sample) / (HOP * tail))
    wave_ref[block(lane), :] = (wave * (ramp_in * ramp_out)).astype(BF16)

    def send(index, peer, send_sem, recv_sem):
        return pltpu.make_async_remote_copy(
            src_ref=wave_ref.at[block(index)],
            dst_ref=wave_ref.at[block(index)],
            send_sem=send_sem,
            recv_sem=recv_sem,
            device_id={"group": peer},
            device_id_type=MESH,
        )

    direct = []
    for step in range(1, chips):
        direct.append(send(lane, ((chip + step) % chips) * 2 + core, wave_send.at[step], wave_recv.at[step]))
        direct[-1].start()
    to_sibling = [send(lane, sibling, fwd_send.at[0], fwd_recv.at[0])]
    to_sibling[0].start()
    for step in range(1, chips):
        direct[step - 1].wait_recv()
        source = ((chip - step + chips) % chips) * 2 + core
        to_sibling.append(send(source, sibling, fwd_send.at[step], fwd_recv.at[step]))
        to_sibling[-1].start()
    for copy in to_sibling:
        copy.wait_recv()
    placed = dot(place_ref[...], wave_ref[...])
    out_ref[pl.ds(0, STR_DEV * SLF, stride=2), :] = placed[:, :128]
    out_ref[pl.ds(1, STR_DEV * SLF, stride=2), :] = placed[:, 128:]
    for copy in direct + to_sibling:
        copy.wait_send()


def shards(
    hidden,
    pre_weight,
    up1_weight,
    up2_weight,
    up3_weight,
    res3_weight,
    up4_weight,
    res4_weight,
    post_weight,
    owner_device,
    stream_slot,
    start_frame,
    lead_frames,
    tail_frames,
):
    sections = lax.axis_size("section")
    lanes = lax.axis_size("group")
    per_device = hidden.shape[0] // sections
    frames, width = hidden.shape[1], hidden.shape[2]
    rows = per_device * frames
    chips = lanes // 2
    total = stream_slot.shape[0]
    vmem = pl.BlockSpec(memory_space=pltpu.VMEM)
    hbm = pl.BlockSpec(memory_space=pltpu.HBM)
    blocks = PAIRS + 2
    out = pl.pallas_call(
        functools.partial(kernel, sections, lanes),
        out_shape=jax.ShapeDtypeStruct((STR_DEV * SLF * HOP // 128, 128), F32),
        in_specs=[hbm] * 4 + [vmem] * 10,
        out_specs=vmem,
        scratch_shapes=[
            pltpu.VMEM((sections * rows, width), BF16),
            pltpu.VMEM(pre_weight.shape, BF16),
            pltpu.VMEM(up1_weight.shape, BF16),
            pltpu.VMEM(up2_weight.shape, BF16),
            pltpu.VMEM((10 * rows, 256), BF16),
            pltpu.VMEM((blocks * rows, 256), BF16),
            pltpu.VMEM((blocks * rows, 256), BF16),
            pltpu.VMEM((PAIRS * rows, 256), F32),
            pltpu.VMEM((512, 256), BF16),
            pltpu.VMEM((768, 256), BF16),
            pltpu.VMEM((512, 256), BF16),
            pltpu.VMEM((512, 256), BF16),
            pltpu.VMEM(((CHUNK * HOP // PAIRS + 8) * 32, 128), BF16),
            pltpu.VMEM((STR_DEV * SLF, lanes * rows), BF16),
            pltpu.VMEM((lanes * rows, HOP), BF16),
            pltpu.SemaphoreType.DMA((3,)),
            pltpu.SemaphoreType.DMA,
            pltpu.SemaphoreType.DMA((sections,)),
            pltpu.SemaphoreType.DMA((sections,)),
            pltpu.SemaphoreType.DMA((chips,)),
            pltpu.SemaphoreType.DMA((chips,)),
            pltpu.SemaphoreType.DMA((chips,)),
            pltpu.SemaphoreType.DMA((chips,)),
        ],
        compiler_params=pltpu.CompilerParams(
            collective_id=0, has_side_effects=True, vmem_limit_bytes=63 * 1024 * 1024
        ),
        name="vocoder",
    )(
        hidden.reshape(sections * rows, width),
        pre_weight,
        up1_weight,
        up2_weight,
        jnp.swapaxes(up3_weight, 1, 2),
        res3_weight,
        jnp.swapaxes(up4_weight, 1, 2),
        res4_weight,
        post_weight,
        owner_device.reshape(1, total),
        stream_slot.reshape(1, total),
        start_frame.reshape(1, total),
        lead_frames.reshape(1, total),
        tail_frames.reshape(1, total),
    )
    return out.reshape(STR_DEV, 1, SLF * HOP)


def solution(mesh):
    in_specs = (P("group", None, "section"),) + (P(),) * 13
    return jax.shard_map(
        shards, mesh=mesh, in_specs=in_specs, out_specs=P("group", "section", None), check_vma=False
    )
```

```python
import functools

import jax
import jax.numpy as jnp
from jax import lax
from jax.experimental import pallas as pl
from jax.experimental.pallas import tpu as pltpu
from jax.sharding import PartitionSpec as P

HOP = 256
STR_DEV = 4
SLF = 64
PAIRS = 32
CHUNK = 8
REACH = 4
PARTS = 2
MESH = pl.DeviceIdType.MESH
F32 = jnp.float32
BF16 = jnp.bfloat16


def leaky(values, slope):
    return jnp.maximum(values, slope * values)


def iota(shape, dim):
    return lax.broadcasted_iota(jnp.int32, shape, dim)


def dot(lhs, rhs):
    return jnp.dot(lhs, rhs, preferred_element_type=F32)


def dot_nt(lhs, rhs):
    return lax.dot_general(lhs, rhs, (((1,), (1,)), ((), ())), preferred_element_type=F32)


def dot_tn(lhs, rhs):
    return lax.dot_general(lhs, rhs, (((0,), (0,)), ((), ())), preferred_element_type=F32)


def shifted(values, step, frames):
    rows = values.shape[0]
    frame = iota(values.shape, 0) & (frames - 1)
    moved = pltpu.roll(values, (-step) % rows, 0)
    inside = (frame + step >= 0) & (frame + step < frames)
    return jnp.where(inside, moved, 0.0)


def assemble(out_ref, spread, times, columns, tap_of):
    depth, width = spread[0].shape
    per_column = width // len(columns)
    column = iota((depth, width), 1) // per_column
    for place, time in enumerate(times):
        block = jnp.zeros((depth, width), F32)
        for at, out_time in enumerate(columns):
            tap = tap_of(time, out_time)
            if tap is not None:
                block = jnp.where(column == at, spread[tap], block)
        out_ref[place * depth : (place + 1) * depth, :] = block.astype(BF16)


def spread_taps(w_ref, copies, flipped):
    taps, width = w_ref.shape[0], w_ref.shape[1 if flipped else 2]
    lanes = width * copies
    repeat = ((iota((width, lanes), 1) & (width - 1)) == iota((width, lanes), 0)).astype(F32).astype(BF16)
    return [(dot_tn if flipped else dot)(w_ref[tap], repeat) for tap in range(taps)]


def up_tap(time, out_time):
    tap = out_time + 1 - 2 * time
    return tap if 0 <= tap < 4 else None


def res_tap(time, out_time):
    step = time - out_time
    return step // 3 + 1 if step in (-3, 0, 3) else None


def kernel(
    sections,
    lanes,
    hidden_ref,
    pre_hbm,
    up1_hbm,
    up2_hbm,
    up3_ref,
    res3_ref,
    up4_ref,
    res4_ref,
    post_ref,
    owner_ref,
    slot_ref,
    start_ref,
    lead_ref,
    tail_ref,
    out_ref,
    x_ref,
    pre_ref,
    up1_ref,
    up2_ref,
    a1_ref,
    a_ref,
    i_ref,
    u_ref,
    w3_ref,
    r3_ref,
    w4_ref,
    r4_ref,
    wp_ref,
    place_ref,
    wave_ref,
    weight_sem,
    own_sem,
    hid_send,
    hid_recv,
    wave_send,
    wave_recv,
    fwd_send,
    fwd_recv,
):
    section = lax.axis_index("section")
    lane = lax.axis_index("group")
    chips = lanes // 2
    chip, core = lane // 2, lane % 2
    sibling = chip * 2 + (1 - core)
    rows = x_ref.shape[0] // sections
    frames = 8
    groups = rows // frames

    def block(index):
        return pl.ds(pl.multiple_of(index * rows, rows), rows)

    pre_taps = pre_ref.shape[0]
    copies = [
        pltpu.make_async_copy(pre_hbm.at[tap], pre_ref.at[tap], weight_sem.at[tap]) for tap in range(pre_taps)
    ]
    copies.append(pltpu.make_async_copy(up1_hbm, up1_ref, weight_sem.at[pre_taps]))
    copies.append(pltpu.make_async_copy(up2_hbm, up2_ref, weight_sem.at[pre_taps + 1]))
    own = pltpu.make_async_copy(hidden_ref.at[block(section)], x_ref.at[block(section)], own_sem)

    barrier = pltpu.get_barrier_semaphore()
    for step in range(1, sections):
        pl.semaphore_signal(
            barrier, inc=1, device_id={"section": (section + step) % sections}, device_id_type=MESH
        )
    for step in range(1, chips):
        pl.semaphore_signal(
            barrier, inc=1, device_id={"group": ((chip + step) % chips) * 2 + core}, device_id_type=MESH
        )
    pl.semaphore_signal(barrier, inc=1, device_id={"group": sibling}, device_id_type=MESH)
    own.start()
    for copy in copies:
        copy.start()
    pl.semaphore_wait(barrier, sections + chips - 1)

    hidden_copies = []
    for step in range(1, sections):
        peer = (section + step) % sections
        hidden_copies.append(
            pltpu.make_async_remote_copy(
                src_ref=hidden_ref.at[block(peer)],
                dst_ref=x_ref.at[block(section)],
                send_sem=hid_send.at[step],
                recv_sem=hid_recv.at[step],
                device_id={"section": peer},
                device_id_type=MESH,
            )
        )
        hidden_copies[-1].start()

    assemble(w3_ref, spread_taps(up3_ref, 4, True), range(-1, 3), range(4), up_tap)
    assemble(r3_ref, spread_taps(res3_ref, 4, False), range(-4, 8), range(4), res_tap)
    assemble(w4_ref, spread_taps(up4_ref, 8, True), range(-2, 6), range(8), up_tap)
    assemble(r4_ref, spread_taps(res4_ref, 8, False), range(-4, 12), range(8), res_tap)
    post = post_ref[...].astype(F32)
    channels = post.shape[1]
    span = REACH * HOP // PAIRS
    eye = (iota((channels, channels), 0) == iota((channels, channels), 1)).astype(F32).astype(BF16)
    post_taps = [
        dot_nt(eye, jnp.broadcast_to(post[tap : tap + 1], (128, channels)).astype(BF16)) for tap in range(7)
    ]
    out_time = iota((channels, 128), 1) & (span - 1)
    for place, time in enumerate(range(-4, span + 4)):
        entry = jnp.zeros((channels, 128), F32)
        for tap in range(7):
            entry = jnp.where(out_time == time - tap + 3, post_taps[tap], entry)
        wp_ref[place * channels : (place + 1) * channels, :] = entry.astype(BF16)

    total = owner_ref.shape[1]
    which = iota((16, total), 0)
    facts = jnp.where(
        which == 0,
        owner_ref[...],
        jnp.where(
            which == 1,
            slot_ref[...] * SLF + start_ref[...],
            jnp.where(which == 2, lead_ref[...], jnp.where(which == 3, tail_ref[...], 0)),
        ),
    )
    facts = facts.astype(F32).astype(BF16)
    lane_groups = sections * groups
    row_group = iota((rows, total), 0) // frames
    mine = (iota((rows, total), 1) == lane * lane_groups + section * groups + row_group).astype(F32).astype(BF16)
    fades = dot_nt(mine, facts)
    lead, tail = fades[:, 2:3], fades[:, 3:4]
    part_rows = rows // PARTS
    column = iota((128, 128), 1)
    column_frame = iota((1, 128), 1) & (frames - 1)
    target_row = iota((STR_DEV * SLF, 128), 0)
    for part in range(PARTS):
        group = part * (groups // PARTS) + (column & (part_rows - 1)) // frames
        pick_row = column // part_rows * lane_groups + section * groups + group
        pick = (iota((128, 128), 0) == pick_row).astype(F32).astype(BF16)
        for tile in range(total // 128):
            found = dot(facts[:, tile * 128 : (tile + 1) * 128], pick)
            owner = found[0:1].astype(jnp.int32)
            target = jnp.where(owner == lane, found[1:2].astype(jnp.int32) + column_frame, -1)
            at = part * lanes * part_rows + tile * 128
            place_ref[:, at : at + 128] = (target_row == target).astype(F32).astype(BF16)

    own.wait()
    for copy in hidden_copies:
        copy.wait()
    x = jnp.concatenate([x_ref[part * rows : (part + 1) * rows, :] for part in range(sections)], axis=1)
    projected = jnp.zeros((rows, pre_ref.shape[2]), F32)
    for tap in range(pre_taps):
        copies[tap].wait()
        projected = projected + shifted(dot(x, pre_ref[tap]), tap - pre_taps // 2, frames)
    active = leaky(projected, 0.1)
    now = active.astype(BF16)
    before = shifted(active, -1, frames).astype(BF16)
    after = shifted(active, 1, frames).astype(BF16)

    copies[pre_taps].wait()
    for phase in range(8):
        other, tap = (before, phase + 12) if phase < 4 else (after, phase - 4)
        up = dot(now, up1_ref[phase + 4]) + dot(other, up1_ref[tap])
        a1_ref[(phase + 1) * rows : (phase + 2) * rows, :] = leaky(up, 0.1).astype(BF16)

    def fill_ends(ref, base, count, depth):
        def at(index):
            return slice(base + index * depth, base + (index + 1) * depth)

        ref[at(0), :] = shifted(ref[at(count), :].astype(F32), -1, frames).astype(BF16)
        ref[at(count + 1), :] = shifted(ref[at(1), :].astype(F32), 1, frames).astype(BF16)

    fill_ends(a1_ref, 0, 8, rows)

    copies[pre_taps + 1].wait()
    for pair in range(4):
        near = 2 * pair + 4
        far, offset = (2 * pair + 12, 0) if pair < 2 else (2 * pair - 4, 2)
        near_w = jnp.concatenate([up2_ref[near], up2_ref[near + 1]], axis=1)
        far_w = jnp.concatenate([up2_ref[far], up2_ref[far + 1]], axis=1)
        for half in range(2):
            low = half * 4
            here = a1_ref[(low + 1) * rows : (low + 5) * rows, :]
            there = a1_ref[(low + offset) * rows : (low + offset + 4) * rows, :]
            up = leaky(dot(here, near_w) + dot(there, far_w), 0.1).astype(BF16)
            for phase in range(4):
                for part in range(PARTS):
                    to = part * (PAIRS + 2) + (low + phase) * 4 + pair + 1
                    a_ref[to * part_rows : (to + 1) * part_rows, :] = up[
                        phase * rows + part * part_rows : phase * rows + (part + 1) * part_rows
                    ]

    size = CHUNK * part_rows

    def around(ref, at, whole):
        low = ref[at : at + size, :]
        mid = ref[at + part_rows : at + part_rows + size, :]
        high = ref[at + 2 * part_rows : at + 2 * part_rows + size, :]
        if not whole:
            low, high = low[:, 128:], high[:, :128]
        return jnp.concatenate([low, mid, high], axis=1)

    def upsample(base, w_ref):
        for at in range(0, PAIRS * part_rows, size):
            up = dot(around(a_ref, base + at, False), w_ref[...])
            u_ref[at : at + size, :] = up
            i_ref[at + part_rows : at + part_rows + size, :] = leaky(up, 0.1).astype(BF16)
        fill_ends(i_ref, 0, PAIRS, part_rows)

    def residual(base, w_ref, whole, slope):
        for at in range(0, PAIRS * part_rows, size):
            middle = u_ref[at : at + size, :] + dot(around(i_ref, at, whole), w_ref[...])
            to = base + part_rows + at
            a_ref[to : to + size, :] = leaky(middle, slope).astype(BF16)
        fill_ends(a_ref, base, PAIRS, part_rows)

    def output(base, part):
        blocks = PAIRS // REACH
        pieces = []
        for piece in range(REACH + 2):
            low, high = (128, 256) if piece == 0 else (0, 128) if piece == REACH + 1 else (0, 256)
            firsts = [base + (at * REACH + piece) * part_rows for at in range(blocks)]
            pieces.append(jnp.concatenate([a_ref[at : at + part_rows, low:high] for at in firsts], axis=0))
        summed = dot(jnp.concatenate(pieces, axis=1), wp_ref[...])
        column = iota((part_rows, 128), 1) // span
        halves = []
        for half in range(HOP // 128):
            merged = jnp.zeros((part_rows, 128), F32)
            for place in range(128 // span):
                first = (half * (128 // span) + place) * part_rows
                merged = jnp.where(column == place, summed[first : first + part_rows], merged)
            halves.append(merged)
        wave = jnp.tanh(jnp.concatenate(halves, axis=1))
        frame = iota((part_rows, HOP), 0) & (frames - 1)
        sample = (frame * HOP + iota((part_rows, HOP), 1)).astype(F32) + 0.5
        here = slice(part * part_rows, (part + 1) * part_rows)
        ramp_in = jnp.minimum(1.0, sample / (HOP * lead[here]))
        ramp_out = jnp.minimum(1.0, (frames * HOP - sample) / (HOP * tail[here]))
        wave_ref[wave_block(part, lane), :] = (wave * (ramp_in * ramp_out)).astype(BF16)

    def wave_block(part, index):
        return pl.ds(pl.multiple_of((part * lanes + index) * part_rows, part_rows), part_rows)

    def send(part, index, peer, send_sem, recv_sem):
        copy = pltpu.make_async_remote_copy(
            src_ref=wave_ref.at[wave_block(part, index)],
            dst_ref=wave_ref.at[wave_block(part, index)],
            send_sem=send_sem,
            recv_sem=recv_sem,
            device_id={"group": peer},
            device_id_type=MESH,
        )
        copy.start()
        return copy

    direct, to_sibling = {}, {}

    def send_wave(part):
        for step in range(1, chips):
            peer = ((chip + step) % chips) * 2 + core
            direct[part, step] = send(part, lane, peer, wave_send.at[part, step], wave_recv.at[part, step])
        to_sibling[part, 0] = send(part, lane, sibling, fwd_send.at[part, 0], fwd_recv.at[part, 0])

    def pass_on(part):
        for step in range(1, chips):
            direct[part, step].wait_recv()
            source = ((chip - step + chips) % chips) * 2 + core
            to_sibling[part, step] = send(
                part, source, sibling, fwd_send.at[part, step], fwd_recv.at[part, step]
            )

    def place(part):
        for step in range(chips):
            to_sibling[part, step].wait_recv()
        span_rows = slice(part * lanes * part_rows, (part + 1) * lanes * part_rows)
        return dot(place_ref[:, span_rows], wave_ref[span_rows, :])

    for part in range(PARTS):
        base = part * (PAIRS + 2) * part_rows
        fill_ends(a_ref, base, PAIRS, part_rows)
        upsample(base, w3_ref)
        residual(base, r3_ref, True, 0.1)
        upsample(base, w4_ref)
        residual(base, r4_ref, False, 0.01)
        if part:
            pass_on(part - 1)
        output(base, part)
        send_wave(part)
    placed = place(0)
    pass_on(PARTS - 1)
    for part in range(1, PARTS):
        placed = placed + place(part)
    out_ref[pl.ds(0, STR_DEV * SLF, stride=2), :] = placed[:, :128]
    out_ref[pl.ds(1, STR_DEV * SLF, stride=2), :] = placed[:, 128:]
    for copy in list(direct.values()) + list(to_sibling.values()):
        copy.wait_send()


def shards(
    hidden,
    pre_weight,
    up1_weight,
    up2_weight,
    up3_weight,
    res3_weight,
    up4_weight,
    res4_weight,
    post_weight,
    owner_device,
    stream_slot,
    start_frame,
    lead_frames,
    tail_frames,
):
    sections = lax.axis_size("section")
    lanes = lax.axis_size("group")
    per_device = hidden.shape[0] // sections
    frames, width = hidden.shape[1], hidden.shape[2]
    rows = per_device * frames
    chips = lanes // 2
    total = stream_slot.shape[0]
    vmem = pl.BlockSpec(memory_space=pltpu.VMEM)
    hbm = pl.BlockSpec(memory_space=pltpu.HBM)
    blocks = PAIRS + 2
    out = pl.pallas_call(
        functools.partial(kernel, sections, lanes),
        out_shape=pltpu.VMEM((STR_DEV * SLF * HOP // 128, 128), F32),
        in_specs=[hbm] * 4 + [vmem] * 10,
        out_specs=vmem,
        scratch_shapes=[
            pltpu.VMEM((sections * rows, width), BF16),
            pltpu.VMEM(pre_weight.shape, BF16),
            pltpu.VMEM(up1_weight.shape, BF16),
            pltpu.VMEM(up2_weight.shape, BF16),
            pltpu.VMEM((10 * rows, 256), BF16),
            pltpu.VMEM((blocks * rows, 256), BF16),
            pltpu.VMEM((blocks * rows // PARTS, 256), BF16),
            pltpu.VMEM((PAIRS * rows // PARTS, 256), F32),
            pltpu.VMEM((512, 256), BF16),
            pltpu.VMEM((768, 256), BF16),
            pltpu.VMEM((512, 256), BF16),
            pltpu.VMEM((512, 256), BF16),
            pltpu.VMEM(((REACH * HOP // PAIRS + 8) * 32, 128), BF16),
            pltpu.VMEM((STR_DEV * SLF, lanes * rows), BF16),
            pltpu.VMEM((lanes * rows, HOP), BF16),
            pltpu.SemaphoreType.DMA((pre_weight.shape[0] + 2,)),
            pltpu.SemaphoreType.DMA,
            pltpu.SemaphoreType.DMA((sections,)),
            pltpu.SemaphoreType.DMA((sections,)),
            pltpu.SemaphoreType.DMA((PARTS, chips)),
            pltpu.SemaphoreType.DMA((PARTS, chips)),
            pltpu.SemaphoreType.DMA((PARTS, chips)),
            pltpu.SemaphoreType.DMA((PARTS, chips)),
        ],
        compiler_params=pltpu.CompilerParams(
            collective_id=0, has_side_effects=True, vmem_limit_bytes=63 * 1024 * 1024
        ),
        name="vocoder",
    )(
        hidden.reshape(sections * rows, width),
        pre_weight,
        up1_weight,
        up2_weight,
        jnp.swapaxes(up3_weight, 1, 2),
        res3_weight,
        jnp.swapaxes(up4_weight, 1, 2),
        res4_weight,
        post_weight,
        owner_device.reshape(1, total),
        stream_slot.reshape(1, total),
        start_frame.reshape(1, total),
        lead_frames.reshape(1, total),
        tail_frames.reshape(1, total),
    )
    return out.reshape(STR_DEV, 1, SLF * HOP)


def solution(mesh):
    in_specs = (P("group", None, "section"),) + (P(),) * 13
    return jax.shard_map(
        shards, mesh=mesh, in_specs=in_specs, out_specs=P("group", "section", None), check_vma=False
    )
```

```python
import functools

import jax
import jax.numpy as jnp
from jax import lax
from jax.experimental import pallas as pl
from jax.experimental.pallas import tpu as pltpu
from jax.sharding import PartitionSpec as P

HOP = 256
STR_DEV = 4
SLF = 64
PAIRS = 32
CHUNK = 4
REACH = 4
PARTS = 2
MESH = pl.DeviceIdType.MESH
F32 = jnp.float32
BF16 = jnp.bfloat16


def leaky(values, slope):
    return jnp.maximum(values, slope * values)


def iota(shape, dim):
    return lax.broadcasted_iota(jnp.int32, shape, dim)


def dot(lhs, rhs):
    return jnp.dot(lhs, rhs, preferred_element_type=F32)


def dot_nt(lhs, rhs):
    return lax.dot_general(lhs, rhs, (((1,), (1,)), ((), ())), preferred_element_type=F32)


def dot_tn(lhs, rhs):
    return lax.dot_general(lhs, rhs, (((0,), (0,)), ((), ())), preferred_element_type=F32)


def shifted(values, step, frames):
    rows = values.shape[0]
    frame = iota(values.shape, 0) & (frames - 1)
    moved = pltpu.roll(values, (-step) % rows, 0)
    inside = (frame + step >= 0) & (frame + step < frames)
    return jnp.where(inside, moved, 0.0)


def assemble(out_ref, spread, times, columns, tap_of):
    depth, width = spread[0].shape
    per_column = width // len(columns)
    column = iota((depth, width), 1) // per_column
    for place, time in enumerate(times):
        block = jnp.zeros((depth, width), F32)
        for at, out_time in enumerate(columns):
            tap = tap_of(time, out_time)
            if tap is not None:
                block = jnp.where(column == at, spread[tap], block)
        out_ref[place * depth : (place + 1) * depth, :] = block.astype(BF16)


def spread_taps(w_ref, copies, flipped):
    taps, width = w_ref.shape[0], w_ref.shape[1 if flipped else 2]
    lanes = width * copies
    repeat = ((iota((width, lanes), 1) & (width - 1)) == iota((width, lanes), 0)).astype(F32).astype(BF16)
    return [(dot_tn if flipped else dot)(w_ref[tap], repeat) for tap in range(taps)]


def up_tap(time, out_time):
    tap = out_time + 1 - 2 * time
    return tap if 0 <= tap < 4 else None


def res_tap(time, out_time):
    step = time - out_time
    return step // 3 + 1 if step in (-3, 0, 3) else None


def kernel(
    sections,
    lanes,
    hidden_ref,
    pre_hbm,
    up1_hbm,
    up2_hbm,
    up3_ref,
    res3_ref,
    up4_ref,
    res4_ref,
    post_ref,
    owner_ref,
    slot_ref,
    start_ref,
    lead_ref,
    tail_ref,
    out_ref,
    x_ref,
    part_ref,
    others_ref,
    pre_ref,
    up1_ref,
    up2_ref,
    a1_ref,
    a_ref,
    i_ref,
    u_ref,
    w3_ref,
    r3_ref,
    w4_ref,
    r4_ref,
    wp_ref,
    place_ref,
    wave_ref,
    weight_sem,
    own_sem,
    hid_send,
    hid_recv,
    wave_send,
    wave_recv,
    fwd_send,
    fwd_recv,
):
    section = lax.axis_index("section")
    lane = lax.axis_index("group")
    chips = lanes // 2
    chip, core = lane // 2, lane % 2
    sibling = chip * 2 + (1 - core)
    rows = x_ref.shape[0] // sections
    frames = 8
    groups = rows // frames

    def block(index):
        return pl.ds(pl.multiple_of(index * rows, rows), rows)

    taps, width = pre_ref.shape[0], pre_ref.shape[1]
    features = pl.ds(pl.multiple_of(section * width, width), width)
    own = pltpu.make_async_copy(hidden_ref, x_ref, own_sem)
    copies = [
        pltpu.make_async_copy(pre_hbm.at[:, features, :], pre_ref, weight_sem.at[0]),
        pltpu.make_async_copy(up1_hbm, up1_ref, weight_sem.at[1]),
        pltpu.make_async_copy(up2_hbm, up2_ref, weight_sem.at[2]),
    ]

    barrier = pltpu.get_barrier_semaphore()
    for step in range(1, sections):
        pl.semaphore_signal(
            barrier, inc=1, device_id={"section": (section + step) % sections}, device_id_type=MESH
        )
    for step in range(1, chips):
        pl.semaphore_signal(
            barrier, inc=1, device_id={"group": ((chip + step) % chips) * 2 + core}, device_id_type=MESH
        )
    pl.semaphore_signal(barrier, inc=1, device_id={"group": sibling}, device_id_type=MESH)
    own.start()
    for copy in copies:
        copy.start()

    own.wait()
    x = x_ref[...].astype(F32)
    windows = jnp.concatenate([shifted(x, tap - taps // 2, frames).astype(BF16) for tap in range(taps)], axis=1)
    copies[0].wait()
    pre_w = pre_ref[...].reshape(taps * width, pre_ref.shape[2])
    everyone = sections * rows
    halves = pre_ref.shape[2] // 256
    for half in range(halves):
        partial = dot(windows, pre_w[:, half * 256 : (half + 1) * 256])
        u_ref[half * everyone : (half + 1) * everyone, :] = partial
        part_ref[:, half * 256 : (half + 1) * 256] = partial.astype(BF16)

    pl.semaphore_wait(barrier, sections + chips - 1)
    partial_copies = []
    for step in range(1, sections):
        peer = (section + step) % sections
        partial_copies.append(
            pltpu.make_async_remote_copy(
                src_ref=part_ref.at[block(peer)],
                dst_ref=others_ref.at[pl.ds((step - 1) * rows, rows)],
                send_sem=hid_send.at[step],
                recv_sem=hid_recv.at[step],
                device_id={"section": peer},
                device_id_type=MESH,
            )
        )
        partial_copies[-1].start()

    assemble(w3_ref, spread_taps(up3_ref, 4, True), range(-1, 3), range(4), up_tap)
    assemble(r3_ref, spread_taps(res3_ref, 4, False), range(-4, 8), range(4), res_tap)
    assemble(w4_ref, spread_taps(up4_ref, 8, True), range(-2, 6), range(8), up_tap)
    assemble(r4_ref, spread_taps(res4_ref, 8, False), range(-4, 12), range(8), res_tap)
    post = post_ref[...].astype(F32)
    channels = post.shape[1]
    span = REACH * HOP // PAIRS
    eye = (iota((channels, channels), 0) == iota((channels, channels), 1)).astype(F32).astype(BF16)
    post_taps = [
        dot_nt(eye, jnp.broadcast_to(post[tap : tap + 1], (128, channels)).astype(BF16)) for tap in range(7)
    ]
    out_time = iota((channels, 128), 1) & (span - 1)
    for place, time in enumerate(range(-4, span + 4)):
        entry = jnp.zeros((channels, 128), F32)
        for tap in range(7):
            entry = jnp.where(out_time == time - tap + 3, post_taps[tap], entry)
        wp_ref[place * channels : (place + 1) * channels, :] = entry.astype(BF16)

    total = owner_ref.shape[1]
    which = iota((16, total), 0)
    facts = jnp.where(
        which == 0,
        owner_ref[...],
        jnp.where(
            which == 1,
            slot_ref[...] * SLF + start_ref[...],
            jnp.where(which == 2, lead_ref[...], jnp.where(which == 3, tail_ref[...], 0)),
        ),
    )
    facts = facts.astype(F32).astype(BF16)
    lane_groups = sections * groups
    row_group = iota((rows, total), 0) // frames
    mine = (iota((rows, total), 1) == lane * lane_groups + section * groups + row_group).astype(F32).astype(BF16)
    fades = dot_nt(mine, facts)
    lead, tail = fades[:, 2:3], fades[:, 3:4]
    part_rows = rows // PARTS
    column = iota((128, 128), 1)
    column_frame = iota((1, 128), 1) & (frames - 1)
    target_row = iota((STR_DEV * SLF, 128), 0)
    for part in range(PARTS):
        group = part * (groups // PARTS) + (column & (part_rows - 1)) // frames
        pick_row = column // part_rows * lane_groups + section * groups + group
        pick = (iota((128, 128), 0) == pick_row).astype(F32).astype(BF16)
        for tile in range(total // 128):
            found = dot(facts[:, tile * 128 : (tile + 1) * 128], pick)
            owner = found[0:1].astype(jnp.int32)
            target = jnp.where(owner == lane, found[1:2].astype(jnp.int32) + column_frame, -1)
            at = part * lanes * part_rows + tile * 128
            place_ref[:, at : at + 128] = (target_row == target).astype(F32).astype(BF16)

    projected = jnp.concatenate(
        [u_ref[pl.ds(pl.multiple_of(half * everyone + section * rows, rows), rows), :] for half in range(halves)],
        axis=1,
    )
    for step in range(1, sections):
        partial_copies[step - 1].wait()
        projected = projected + others_ref[(step - 1) * rows : step * rows, :].astype(F32)
    active = leaky(projected, 0.1)
    now = active.astype(BF16)
    before = shifted(active, -1, frames).astype(BF16)
    after = shifted(active, 1, frames).astype(BF16)

    copies[1].wait()
    for phase in range(8):
        other, tap = (before, phase + 12) if phase < 4 else (after, phase - 4)
        up = dot(now, up1_ref[phase + 4]) + dot(other, up1_ref[tap])
        a1_ref[(phase + 1) * rows : (phase + 2) * rows, :] = leaky(up, 0.1).astype(BF16)

    def fill_before(ref, count):
        last = ref[count * rows : (count + 1) * rows, :].astype(F32)
        ref[0:rows, :] = shifted(last, -1, frames).astype(BF16)

    def fill_after(ref, count):
        first = ref[rows : 2 * rows, :].astype(F32)
        ref[(count + 1) * rows : (count + 2) * rows, :] = shifted(first, 1, frames).astype(BF16)

    fill_before(a1_ref, 8)
    fill_after(a1_ref, 8)

    copies[2].wait()
    for pair in range(4):
        near = 2 * pair + 4
        far, offset = (2 * pair + 12, 0) if pair < 2 else (2 * pair - 4, 2)
        near_w = jnp.concatenate([up2_ref[near], up2_ref[near + 1]], axis=1)
        far_w = jnp.concatenate([up2_ref[far], up2_ref[far + 1]], axis=1)
        for half in range(2):
            low = half * 4
            here = a1_ref[(low + 1) * rows : (low + 5) * rows, :]
            there = a1_ref[(low + offset) * rows : (low + offset + 4) * rows, :]
            up = leaky(dot(here, near_w) + dot(there, far_w), 0.1).astype(BF16)
            for phase in range(4):
                to = (low + phase) * 4 + pair + 1
                a_ref[to * rows : (to + 1) * rows, :] = up[phase * rows : (phase + 1) * rows]
    fill_before(a_ref, PAIRS)
    fill_after(a_ref, PAIRS)

    def level(first, ref, body):
        chunks = PAIRS // CHUNK
        for turn in range(chunks):
            chunk = (first + turn) % chunks
            body(chunk * CHUNK)
            if chunk == chunks - 1:
                fill_before(ref, PAIRS)
            if chunk == 0:
                fill_after(ref, PAIRS)

    def around(ref, at, whole):
        size = CHUNK * rows
        low, mid, high = (ref[(at + shift) * rows : (at + shift) * rows + size, :] for shift in range(3))
        if not whole:
            low, high = low[:, 128:], high[:, :128]
        return jnp.concatenate([low, mid, high], axis=1)

    def upsample(first, w_ref):
        def body(at):
            up = dot(around(a_ref, at, False), w_ref[...])
            u_ref[at * rows : (at + CHUNK) * rows, :] = up
            i_ref[(at + 1) * rows : (at + 1 + CHUNK) * rows, :] = leaky(up, 0.1).astype(BF16)

        level(first, i_ref, body)

    def residual(first, w_ref):
        def body(at):
            middle = u_ref[at * rows : (at + CHUNK) * rows, :] + dot(around(i_ref, at, True), w_ref[...])
            a_ref[(at + 1) * rows : (at + 1 + CHUNK) * rows, :] = leaky(middle, 0.1).astype(BF16)

        level(first, a_ref, body)

    def gathered(ref, blocks, part, low, high):
        starts = [index * rows + part * part_rows for index in blocks]
        return jnp.concatenate([ref[at : at + part_rows, low:high] for at in starts], axis=0)

    def last_residual(first, part):
        count = CHUNK * PARTS
        chunks = PAIRS // count
        for turn in range(chunks):
            at = (first + turn) % chunks * count
            lhs = jnp.concatenate(
                [
                    gathered(i_ref, range(at, at + count), part, 128, 256),
                    gathered(i_ref, range(at + 1, at + 1 + count), part, 0, 256),
                    gathered(i_ref, range(at + 2, at + 2 + count), part, 0, 128),
                ],
                axis=1,
            )
            middle = gathered(u_ref, range(at, at + count), part, 0, 256) + dot(lhs, r4_ref[...])
            result = leaky(middle, 0.01).astype(BF16)
            for index in range(count):
                to = (at + 1 + index) * rows + part * part_rows
                a_ref[to : to + part_rows, :] = result[index * part_rows : (index + 1) * part_rows]
        low = part * part_rows
        last = a_ref[PAIRS * rows + low : PAIRS * rows + low + part_rows, :].astype(F32)
        a_ref[low : low + part_rows, :] = shifted(last, -1, frames).astype(BF16)
        start = a_ref[rows + low : rows + low + part_rows, :].astype(F32)
        end = (PAIRS + 1) * rows + low
        a_ref[end : end + part_rows, :] = shifted(start, 1, frames).astype(BF16)

    def output(part):
        pieces = []
        for piece in range(REACH + 2):
            low, high = (128, 256) if piece == 0 else (0, 128) if piece == REACH + 1 else (0, 256)
            pieces.append(gathered(a_ref, range(piece, piece + PAIRS, REACH), part, low, high))
        summed = dot(jnp.concatenate(pieces, axis=1), wp_ref[...])
        column = iota((part_rows, 128), 1) // span
        halves = []
        for half in range(HOP // 128):
            merged = jnp.zeros((part_rows, 128), F32)
            for place in range(128 // span):
                first = (half * (128 // span) + place) * part_rows
                merged = jnp.where(column == place, summed[first : first + part_rows], merged)
            halves.append(merged)
        wave = jnp.tanh(jnp.concatenate(halves, axis=1))
        frame = iota((part_rows, HOP), 0) & (frames - 1)
        sample = (frame * HOP + iota((part_rows, HOP), 1)).astype(F32) + 0.5
        here = slice(part * part_rows, (part + 1) * part_rows)
        ramp_in = jnp.minimum(1.0, sample / (HOP * lead[here]))
        ramp_out = jnp.minimum(1.0, (frames * HOP - sample) / (HOP * tail[here]))
        wave_ref[wave_block(part, lane), :] = (wave * (ramp_in * ramp_out)).astype(BF16)

    def wave_block(part, index):
        return pl.ds(pl.multiple_of((part * lanes + index) * part_rows, part_rows), part_rows)

    def send(part, index, peer, send_sem, recv_sem):
        copy = pltpu.make_async_remote_copy(
            src_ref=wave_ref.at[wave_block(part, index)],
            dst_ref=wave_ref.at[wave_block(part, index)],
            send_sem=send_sem,
            recv_sem=recv_sem,
            device_id={"group": peer},
            device_id_type=MESH,
        )
        copy.start()
        return copy

    direct, to_sibling = {}, {}

    def send_wave(part):
        for step in range(1, chips):
            peer = ((chip + step) % chips) * 2 + core
            direct[part, step] = send(part, lane, peer, wave_send.at[part, step], wave_recv.at[part, step])
        to_sibling[part, 0] = send(part, lane, sibling, fwd_send.at[part, 0], fwd_recv.at[part, 0])

    def pass_on(part):
        for step in range(1, chips):
            direct[part, step].wait_recv()
            source = ((chip - step + chips) % chips) * 2 + core
            to_sibling[part, step] = send(
                part, source, sibling, fwd_send.at[part, step], fwd_recv.at[part, step]
            )

    def place(part):
        for step in range(chips):
            to_sibling[part, step].wait_recv()
        span_rows = slice(part * lanes * part_rows, (part + 1) * lanes * part_rows)
        return dot(place_ref[:, span_rows], wave_ref[span_rows, :])

    upsample(0, w3_ref)
    residual(1, r3_ref)
    upsample(2, w4_ref)
    for part in range(PARTS):
        last_residual(2, part)
        output(part)
        send_wave(part)
    pass_on(0)
    placed = place(0)
    pass_on(PARTS - 1)
    for part in range(1, PARTS):
        placed = placed + place(part)
    out_ref[pl.ds(0, STR_DEV * SLF, stride=2), :] = placed[:, :128]
    out_ref[pl.ds(1, STR_DEV * SLF, stride=2), :] = placed[:, 128:]
    for copy in list(direct.values()) + list(to_sibling.values()):
        copy.wait_send()


def shards(
    hidden,
    pre_weight,
    up1_weight,
    up2_weight,
    up3_weight,
    res3_weight,
    up4_weight,
    res4_weight,
    post_weight,
    owner_device,
    stream_slot,
    start_frame,
    lead_frames,
    tail_frames,
):
    sections = lax.axis_size("section")
    lanes = lax.axis_size("group")
    per_device = hidden.shape[0] // sections
    frames, width = hidden.shape[1], hidden.shape[2]
    rows = per_device * frames
    chips = lanes // 2
    total = stream_slot.shape[0]
    vmem = pl.BlockSpec(memory_space=pltpu.VMEM)
    hbm = pl.BlockSpec(memory_space=pltpu.HBM)
    blocks = PAIRS + 2
    out = pl.pallas_call(
        functools.partial(kernel, sections, lanes),
        out_shape=pltpu.VMEM((STR_DEV * SLF * HOP // 128, 128), F32),
        in_specs=[hbm] * 4 + [vmem] * 10,
        out_specs=vmem,
        scratch_shapes=[
            pltpu.VMEM((sections * rows, width), BF16),
            pltpu.VMEM((sections * rows, pre_weight.shape[2]), BF16),
            pltpu.VMEM(((sections - 1) * rows, pre_weight.shape[2]), BF16),
            pltpu.VMEM((pre_weight.shape[0], width, pre_weight.shape[2]), BF16),
            pltpu.VMEM(up1_weight.shape, BF16),
            pltpu.VMEM(up2_weight.shape, BF16),
            pltpu.VMEM((10 * rows, 256), BF16),
            pltpu.VMEM((blocks * rows, 256), BF16),
            pltpu.VMEM((blocks * rows, 256), BF16),
            pltpu.VMEM((PAIRS * rows, 256), F32),
            pltpu.VMEM((512, 256), BF16),
            pltpu.VMEM((768, 256), BF16),
            pltpu.VMEM((512, 256), BF16),
            pltpu.VMEM((512, 256), BF16),
            pltpu.VMEM(((REACH * HOP // PAIRS + 8) * 32, 128), BF16),
            pltpu.VMEM((STR_DEV * SLF, lanes * rows), BF16),
            pltpu.VMEM((lanes * rows, HOP), BF16),
            pltpu.SemaphoreType.DMA((3,)),
            pltpu.SemaphoreType.DMA,
            pltpu.SemaphoreType.DMA((sections,)),
            pltpu.SemaphoreType.DMA((sections,)),
            pltpu.SemaphoreType.DMA((PARTS, chips)),
            pltpu.SemaphoreType.DMA((PARTS, chips)),
            pltpu.SemaphoreType.DMA((PARTS, chips)),
            pltpu.SemaphoreType.DMA((PARTS, chips)),
        ],
        compiler_params=pltpu.CompilerParams(
            collective_id=0, has_side_effects=True, vmem_limit_bytes=63 * 1024 * 1024
        ),
        name="vocoder",
    )(
        hidden.reshape(sections * rows, width),
        pre_weight,
        up1_weight,
        up2_weight,
        jnp.swapaxes(up3_weight, 1, 2),
        res3_weight,
        jnp.swapaxes(up4_weight, 1, 2),
        res4_weight,
        post_weight,
        owner_device.reshape(1, total),
        stream_slot.reshape(1, total),
        start_frame.reshape(1, total),
        lead_frames.reshape(1, total),
        tail_frames.reshape(1, total),
    )
    return out.reshape(STR_DEV, 1, SLF * HOP)


def solution(mesh):
    in_specs = (P("group", None, "section"),) + (P(),) * 13
    return jax.shard_map(
        shards, mesh=mesh, in_specs=in_specs, out_specs=P("group", "section", None), check_vma=False
    )
```
